32 devices in a mesh: grp: 2 (over x), row: 16 (over z, y, core).
Axes of the slice: x: 2, y: 2, z: 4, core: 2. Of those that a mesh axis runs over, the one named last changes fastest.
Arguments:
- stacked_homolog_states: bfloat16 [128, 256, 256], P('grp', 'row'), parts along dimension 0, may hold values from -6 to 6
- pairwise_activations: bfloat16 [512, 256, 128], P(('grp', 'row')), parts along dimension 0, may hold values from -6 to 6
- normalizer_factor: float32 [256], replicated, may hold values from 0.1 to 1.9
- normalizer_shift: float32 [256], replicated, may hold values from -3 to 3
- former_linear_matrix: bfloat16 [256, 32], replicated, may hold values from -0.375 to 0.375
- left_projection_bias: float32 [32], replicated, may hold values from -3 to 3
- latter_linear_matrix: bfloat16 [256, 32], replicated, may hold values from -0.375 to 0.375
- right_projection_bias: float32 [32], replicated, may hold values from -3 to 3
- output_projection_weight: bfloat16 [1024, 128], replicated, may hold values from -0.75 to 0.75
- output_bias_vector: float32 [128], replicated, may hold values from -3 to 3
Outputs:
- pair_rows: bfloat16 [512, 256, 128], P(('grp', 'row')), parts along dimension 0
- pair_cols: bfloat16 [512, 256, 128], P(('grp', 'row')), parts along dimension 0
The draws below stay inside these ranges and needn't reach their ends.
There are 2 independent parts, one for each index of `grp`. The reference program is written for one: setup_inputs(seed, part) draws one part's arguments, and reference() takes and returns one part's arrays. A program takes and returns all parts, laid end to end along the dimension named above; an argument that names none is the same for every part. Nothing has to cross between parts.
All inputs are finite; a program needn't handle non-finite values.
Results may differ from the reference program's by a relative error of at most 0.0053.
Values may be sent and summed in bfloat16 or wider, within the bound.
No kernel may reach another device: no remote copies, remote signals or barrier semaphores. Data moves between devices by JAX's collectives and lax.ppermute only.
A program may use at most 128 MiB of HBM per device.

```python
import jax
import jax.numpy as jnp
from jax import lax

FEATURE_DEPTH = 256
HIDDEN_FEATURES = 32
C_Z = 128
SUBSET_ROW_COUNT = 64
ROWS_DEV = 16
AMINO_SPAN = 256


def levels(key, dims, pieces, smallest, largest):
    gain, own = 1.0, jax.random.fold_in(key, 6)
    for position, shards_of in pieces:
        heights = jnp.exp(jax.random.uniform(jax.random.fold_in(own, position), (shards_of,), jnp.float32, smallest / len(pieces), largest / len(pieces)))
        gain = gain * jnp.repeat(heights, dims[position] // shards_of).reshape([-1 if axis == position else 1 for axis in range(len(dims))])
    return gain


def normal_values(key, extent, scale, limit, split=(), kind=jnp.bfloat16):
    loudness = levels(key, extent, split, -0.22, 0.18) if split else 1.0
    entries = jax.random.normal(key, extent, jnp.float32) * scale * loudness
    return jnp.minimum(jnp.maximum(entries, -limit), limit).astype(kind)


def setup_inputs(seed: int = 0, part: int = 0) -> dict:
    keys = jax.random.split(jax.random.key(seed), 11)
    own_keys = jax.random.split(jax.random.fold_in(keys[10], part), 11)
    return {
        "stacked_homolog_states": normal_values(own_keys[0], (SUBSET_ROW_COUNT, AMINO_SPAN, FEATURE_DEPTH), 1.0, 6.0, ((1, 16),)),
        "pairwise_activations": normal_values(own_keys[1], (AMINO_SPAN, AMINO_SPAN, C_Z), 1.0, 6.0, ((0, 16),)),
        "normalizer_factor": jnp.clip(1.0 + 0.18 * jax.random.normal(keys[2], (FEATURE_DEPTH,), jnp.float32), 0.1, 1.9),
        "normalizer_shift": normal_values(keys[3], (FEATURE_DEPTH,), 0.5, 3.0, (), jnp.float32),
        "former_linear_matrix": normal_values(keys[4], (FEATURE_DEPTH, HIDDEN_FEATURES), FEATURE_DEPTH ** -0.5, 0.375),
        "left_projection_bias": normal_values(keys[5], (HIDDEN_FEATURES,), 0.5, 3.0, (), jnp.float32),
        "latter_linear_matrix": normal_values(keys[6], (FEATURE_DEPTH, HIDDEN_FEATURES), FEATURE_DEPTH ** -0.5, 0.375),
        "right_projection_bias": normal_values(keys[7], (HIDDEN_FEATURES,), 0.5, 3.0, (), jnp.float32),
        "output_projection_weight": normal_values(keys[8], (HIDDEN_FEATURES * HIDDEN_FEATURES, C_Z), (HIDDEN_FEATURES * HIDDEN_FEATURES // 16) ** -0.5, 0.75),
        "output_bias_vector": normal_values(keys[9], (C_Z,), 0.5, 3.0, (), jnp.float32),
    }


def project_alignment(stacked_homolog_states, normalizer_factor, normalizer_shift, former_linear_matrix, left_projection_bias, latter_linear_matrix, right_projection_bias):
    outer_value_grid = stacked_homolog_states.astype(jnp.float32)
    center = lax.optimization_barrier(jnp.mean(outer_value_grid, axis=-1, keepdims=True))
    spread = lax.optimization_barrier(jnp.mean((outer_value_grid - center) ** 2, axis=-1, keepdims=True))
    normed = ((outer_value_grid - center) * lax.rsqrt(spread + 1e-05) * normalizer_factor + normalizer_shift).astype(jnp.bfloat16)
    left_activations = (jnp.dot(normed, former_linear_matrix, preferred_element_type=jnp.float32) + left_projection_bias).astype(jnp.bfloat16)
    right_activations = (jnp.dot(normed, latter_linear_matrix, preferred_element_type=jnp.float32) + right_projection_bias).astype(jnp.bfloat16)
    return (left_activations, right_activations)

def reference(stacked_homolog_states, pairwise_activations, normalizer_factor, normalizer_shift, former_linear_matrix, left_projection_bias, latter_linear_matrix, right_projection_bias, output_projection_weight, output_bias_vector):
    left_activations, right_activations = project_alignment(stacked_homolog_states, normalizer_factor, normalizer_shift, former_linear_matrix, left_projection_bias, latter_linear_matrix, right_projection_bias)
    blocks = AMINO_SPAN // ROWS_DEV

    def one_block(block_id):
        start = (block_id * ROWS_DEV).astype(jnp.int32)
        first_rows = lax.dynamic_slice_in_dim(left_activations, start, ROWS_DEV, 1)
        pair_rows = lax.dynamic_slice_in_dim(pairwise_activations, start, ROWS_DEV, 0)
        outer = jnp.einsum('sic,sjd->ijcd', first_rows.astype(jnp.float32), right_activations.astype(jnp.float32))
        outer = (outer * (1.0 / SUBSET_ROW_COUNT)).astype(jnp.bfloat16)
        flat = outer.reshape(ROWS_DEV * AMINO_SPAN, HIDDEN_FEATURES * HIDDEN_FEATURES)
        update = jnp.dot(flat, output_projection_weight, preferred_element_type=jnp.float32) + output_bias_vector
        return (pair_rows + update.reshape(ROWS_DEV, AMINO_SPAN, C_Z)).astype(jnp.bfloat16)
    result = lax.map(one_block, jnp.arange(blocks, dtype=jnp.int32))
    result = result.reshape(AMINO_SPAN, AMINO_SPAN, C_Z)
    return (result, jnp.swapaxes(result, 0, 1))
```

```python
import functools

import jax
import jax.numpy as jnp
from jax import lax
from jax.experimental import pallas as pl
from jax.experimental.pallas import tpu as pltpu
from jax.sharding import PartitionSpec as P

LANES = 128
MIB = 1 << 20


def _cost(flops, nbytes):
    return pl.CostEstimate(flops=flops, bytes_accessed=nbytes, transcendentals=0)


def _project_kernel(x_ref, g_ref, b_ref, wt_ref, pb_ref, local_ref, first_ref, second_ref, proj, turned):
    seqs, rows, depth = x_ref.shape
    hidden = wt_ref.shape[0] // 2
    half = hidden // 2
    step = 8
    for s in range(0, seqs, step):
        x = x_ref[s : s + step].astype(jnp.float32).reshape(step * rows, depth)
        center = jnp.mean(x, axis=-1, keepdims=True)
        x = x - center
        spread = jnp.mean(x * x, axis=-1, keepdims=True)
        normed = (x * lax.rsqrt(spread + 1e-05) * g_ref[...] + b_ref[...]).astype(jnp.bfloat16)
        y = lax.dot_general(normed, wt_ref[...], (((1,), (1,)), ((), ())), preferred_element_type=jnp.float32)
        y = (y + pb_ref[...]).astype(jnp.bfloat16).astype(jnp.float32)
        proj[s * rows : (s + step) * rows, :] = jnp.concatenate(
            [y, jnp.zeros((step * rows, LANES - 2 * hidden), jnp.float32)], axis=1
        )
    pair = LANES // seqs
    for i in range(0, rows, pair):
        parts = [proj[pl.ds(i + p, seqs, stride=rows), :] for p in range(pair)]
        for p in range(pair):
            local_ref[i + p] = parts[p][:, : 2 * hidden].astype(jnp.bfloat16)
        t = jnp.concatenate(parts, axis=0).T
        for p in range(pair):
            cols = slice(p * seqs, (p + 1) * seqs)
            for which in range(2):
                base = which * hidden
                z = jnp.concatenate([t[base : base + half, cols], t[base + half : base + hidden, cols]], axis=1)
                turned[which, (i + p) * half : (i + p + 1) * half, :] = z
    for r in range(half):
        first_ref[:, r * LANES : (r + 1) * LANES] = turned[0, pl.ds(r, rows, stride=half), :].astype(jnp.bfloat16)
        second_ref[:, r * LANES : (r + 1) * LANES] = turned[1, pl.ds(r, rows, stride=half), :].astype(jnp.bfloat16)


def project(x, g, b, wt, pb):
    seqs, rows, depth = x.shape
    hidden = wt.shape[0] // 2
    flat = jax.ShapeDtypeStruct((rows, hidden * seqs), jnp.bfloat16)
    return pl.pallas_call(
        _project_kernel,
        out_shape=(jax.ShapeDtypeStruct((rows, seqs, 2 * hidden), jnp.bfloat16), flat, flat),
        scratch_shapes=[
            pltpu.VMEM((seqs * rows, LANES), jnp.float32),
            pltpu.VMEM((2, rows * hidden // 2, LANES), jnp.float32),
        ],
        compiler_params=pltpu.CompilerParams(vmem_limit_bytes=24 * MIB),
        cost_estimate=_cost(4_000_000_000, 2_000_000),
        name="project",
    )(x, g, b, wt, pb)


def _spread_kernel(local_ref, w_ref, t_ref, u_ref, wf):
    rows, seqs, both = local_ref.shape
    hidden = both // 2
    half = hidden // 2
    width = w_ref.shape[1]
    wf[...] = w_ref[...].astype(jnp.float32)
    blank = jnp.zeros((hidden, 2 * width), jnp.float32)
    group = 256 // seqs
    for r in range(half):
        wt = jnp.concatenate([wf[pl.ds(r, hidden, stride=hidden), :], wf[pl.ds(r + half, hidden, stride=hidden), :]], axis=1)
        wu = jnp.concatenate([wf[r * hidden : (r + 1) * hidden, :], wf[(r + half) * hidden : (r + half + 1) * hidden, :]], axis=1)
        wt = jnp.concatenate([wt, blank], axis=0).astype(jnp.bfloat16)
        wu = jnp.concatenate([blank, wu], axis=0).astype(jnp.bfloat16)
        for i in range(0, rows, group):
            a = local_ref[i : i + group].reshape(group * seqs, both)
            for out_ref, w in ((t_ref, wt), (u_ref, wu)):
                y = jnp.dot(a, w, preferred_element_type=jnp.float32).astype(jnp.bfloat16)
                for k in range(group):
                    for h in range(2):
                        out_ref[
                            (i + k) // 2,
                            (2 * r + h) * seqs : (2 * r + h + 1) * seqs,
                            (k % 2) * width : (k % 2 + 1) * width,
                        ] = y[k * seqs : (k + 1) * seqs, h * width : (h + 1) * width]


def spread_weights(local, w):
    rows, seqs, both = local.shape
    hidden = both // 2
    width = w.shape[1]
    out = jax.ShapeDtypeStruct((rows // 2, hidden * seqs, 2 * width), jnp.bfloat16)
    return pl.pallas_call(
        _spread_kernel,
        out_shape=(out, out),
        scratch_shapes=[pltpu.VMEM(w.shape, jnp.float32)],
        compiler_params=pltpu.CompilerParams(vmem_limit_bytes=48 * MIB),
        cost_estimate=_cost(6_000_000_000, 17_000_000),
        name="spread_weights",
    )(local, w)


def _gather_rows(me, order, pieces, whole):
    rows = pieces[0].shape[0]
    for k, piece in zip(order, pieces):
        at = pl.multiple_of((me ^ k) * rows, rows)
        whole[pl.ds(at, rows), :] = piece[...]


def _rows_kernel(order, scale, me_ref, bias_ref, pair_ref, t_ref, *refs):
    pieces, out_ref, whole = refs[: len(order)], refs[-2], refs[-1]

    @pl.when(pl.program_id(0) == 0)
    def _():
        _gather_rows(me_ref[0], order, pieces, whole)

    width = bias_ref.shape[1]
    y = jnp.dot(whole[...], t_ref[0], preferred_element_type=jnp.float32)
    for k in range(2):
        up = y[:, k * width : (k + 1) * width] * scale + bias_ref[...]
        out_ref[k] = (pair_ref[k].astype(jnp.float32) + up).astype(jnp.bfloat16)


def update_rows(me, order, scale, bias, pair, t, pieces):
    rows, span, width = pair.shape
    own, inner = pieces[0].shape
    return pl.pallas_call(
        functools.partial(_rows_kernel, order, scale),
        grid=(rows // 2,),
        in_specs=[
            pl.BlockSpec(memory_space=pltpu.SMEM),
            pl.BlockSpec((1, width), lambda i: (0, 0)),
            pl.BlockSpec((2, span, width), lambda i: (i, 0, 0)),
            pl.BlockSpec((1, inner, 2 * width), lambda i: (i, 0, 0)),
        ]
        + [pl.BlockSpec((own, inner), lambda i: (0, 0))] * len(order),
        out_specs=pl.BlockSpec((2, span, width), lambda i: (i, 0, 0)),
        out_shape=jax.ShapeDtypeStruct(pair.shape, jnp.bfloat16),
        scratch_shapes=[pltpu.VMEM((span, inner), jnp.bfloat16)],
        compiler_params=pltpu.CompilerParams(vmem_limit_bytes=48 * MIB),
        cost_estimate=_cost(3_000_000_000, 12_000_000),
        name="update_rows",
    )(me, bias, pair, t, *pieces)


def _cols_kernel(order, scale, me_ref, bias_ref, got_ref, t_ref, *refs):
    pieces, out_ref, whole, turned = refs[: len(order)], refs[-3], refs[-2], refs[-1]
    count, rows, _, width = got_ref.shape

    @pl.when(pl.program_id(0) == 0)
    def _():
        _gather_rows(me_ref[0], order, pieces, whole)
        n = rows * rows
        a = lax.broadcasted_iota(jnp.int32, (n, n), 0)
        b = lax.broadcasted_iota(jnp.int32, (n, n), 1)
        swap = ((a % rows) * rows + a // rows == b).astype(jnp.bfloat16)
        for c in range(count):
            y = jnp.dot(swap, got_ref[c].reshape(n, width), preferred_element_type=jnp.float32)
            turned[:, c * rows : (c + 1) * rows, :] = y.astype(jnp.bfloat16).reshape(rows, rows, width)

    y = jnp.dot(whole[...], t_ref[0], preferred_element_type=jnp.float32)
    i = pl.program_id(0)
    for k in range(2):
        up = y[:, k * width : (k + 1) * width] * scale + bias_ref[...]
        out_ref[k] = (turned[2 * i + k].astype(jnp.float32) + up).astype(jnp.bfloat16)


def update_cols(me, order, scale, bias, got, t, pieces):
    count, rows, _, width = got.shape
    span = count * rows
    own, inner = pieces[0].shape
    return pl.pallas_call(
        functools.partial(_cols_kernel, order, scale),
        grid=(rows // 2,),
        in_specs=[
            pl.BlockSpec(memory_space=pltpu.SMEM),
            pl.BlockSpec((1, width), lambda i: (0, 0)),
            pl.BlockSpec(got.shape, lambda i: (0, 0, 0, 0)),
            pl.BlockSpec((1, inner, 2 * width), lambda i: (i, 0, 0)),
        ]
        + [pl.BlockSpec((own, inner), lambda i: (0, 0))] * len(order),
        out_specs=pl.BlockSpec((2, span, width), lambda i: (i, 0, 0)),
        out_shape=jax.ShapeDtypeStruct((rows, span, width), jnp.bfloat16),
        scratch_shapes=[pltpu.VMEM((span, inner), jnp.bfloat16), pltpu.VMEM((rows, span, width), jnp.bfloat16)],
        compiler_params=pltpu.CompilerParams(vmem_limit_bytes=56 * MIB),
        cost_estimate=_cost(3_000_000_000, 12_000_000),
        name="update_cols",
    )(me, bias, got, t, *pieces)


def gather_pieces(x, n):
    pieces, order = [x], [0]
    k = n // 2
    while k:
        pairs = [(i, i ^ k) for i in range(n)]
        pieces = pieces + [lax.ppermute(p, "row", pairs) for p in pieces]
        order = order + [o ^ k for o in order]
        k //= 2
    return pieces, tuple(order)


def body(n, x, pair, g, b, w1, b1, w2, b2, w, bias):
    seqs, rows, depth = x.shape
    width = pair.shape[-1]
    me = lax.axis_index("row").astype(jnp.int32).reshape(1)
    wt = jnp.concatenate([w1.T, w2.T], axis=0)
    pb = jnp.concatenate([b1, b2]).reshape(1, -1)
    blocks = pair.reshape(rows, n, rows, width).transpose(1, 0, 2, 3)
    got = lax.all_to_all(blocks, "row", split_axis=0, concat_axis=0, tiled=True)
    local, first, second = project(x, g.reshape(1, depth), b.reshape(1, depth), wt, pb)
    seconds, order = gather_pieces(second, n)
    firsts, _ = gather_pieces(first, n)
    t, u = spread_weights(local, w)
    scale = 1.0 / seqs
    bias = bias.reshape(1, width)
    pair_rows = update_rows(me, order, scale, bias, pair, t, seconds)
    pair_cols = update_cols(me, order, scale, bias, got, u, firsts)
    return pair_rows, pair_cols


def solution(mesh):
    pair_spec = P(("grp", "row"), None, None)
    in_specs = (P("grp", "row", None), pair_spec) + (P(),) * 8
    return jax.shard_map(
        functools.partial(body, mesh.shape["row"]),
        mesh=mesh,
        in_specs=in_specs,
        out_specs=(pair_spec, pair_spec),
        check_vma=False,
    )
```

```python
import functools

import jax
import jax.numpy as jnp
from jax import lax
from jax.experimental import pallas as pl
from jax.experimental.pallas import tpu as pltpu
from jax.sharding import PartitionSpec as P

LANES = 128
MIB = 1 << 20
ANY = pl.BlockSpec(memory_space=pl.ANY)
VMEM = pl.BlockSpec(memory_space=pltpu.VMEM)
SMEM = pl.BlockSpec(memory_space=pltpu.SMEM)


def _cost(flops, nbytes):
    return pl.CostEstimate(flops=flops, bytes_accessed=nbytes, transcendentals=0)


def _project_kernel(
    n, x_hbm, pair_hbm, g_hbm, b_hbm, w1_hbm, c1_hbm, w2_hbm, c2_hbm, w_hbm, local_ref, flat_ref, out_w_ref, mine_ref, theirs_ref, *refs
):
    x_ref, pair_ref, g_ref, b_ref, w_ref, c_ref, proj, turned, in_sem, x_sem, sem = refs
    me = lax.axis_index("row")
    seqs, rows, depth = x_ref.shape
    hidden = w_ref.shape[0] // 2
    half = hidden // 2
    step = 8
    loads = [
        pltpu.make_async_copy(src, dst, in_sem.at[k])
        for k, (src, dst) in enumerate(
            (
                (g_hbm, g_ref),
                (b_hbm, b_ref),
                (w1_hbm, w_ref.at[pl.ds(0, hidden), :]),
                (w2_hbm, w_ref.at[pl.ds(hidden, hidden), :]),
                (c1_hbm, c_ref.at[0]),
                (c2_hbm, c_ref.at[1]),
            )
        )
    ]
    part = seqs // 2
    chunks = [
        pltpu.make_async_copy(x_hbm.at[pl.ds(k * part, part)], x_ref.at[pl.ds(k * part, part)], x_sem.at[k])
        for k in range(2)
    ]
    others = [pltpu.make_async_copy(pair_hbm, pair_ref, sem.at[0]), pltpu.make_async_copy(w_hbm, out_w_ref, sem.at[1])]
    for c in chunks[:1] + loads + chunks[1:] + others:
        c.start()
    for c in loads:
        c.wait()
    bias = jnp.concatenate([c_ref[0], c_ref[1]], axis=1)
    for s in range(0, seqs, step):
        if s % part == 0:
            chunks[s // part].wait()
        x = x_ref[s : s + step].astype(jnp.float32).reshape(step * rows, depth)
        center = jnp.mean(x, axis=-1, keepdims=True)
        x = x - center
        spread = jnp.mean(x * x, axis=-1, keepdims=True)
        normed = (x * lax.rsqrt(spread + 1e-05) * g_ref[...] + b_ref[...]).astype(jnp.bfloat16)
        y = lax.dot_general(normed, w_ref[...], (((1,), (1,)), ((), ())), preferred_element_type=jnp.float32)
        y = (y + bias).astype(jnp.bfloat16).astype(jnp.float32)
        proj[s * rows : (s + step) * rows, :] = jnp.concatenate(
            [y, jnp.zeros((step * rows, LANES - 2 * hidden), jnp.float32)], axis=1
        )
    pack = LANES // seqs
    for i in range(0, rows, pack):
        parts = [proj[pl.ds(i + p, seqs, stride=rows), :] for p in range(pack)]
        for p in range(pack):
            local_ref[i + p] = parts[p][:, : 2 * hidden].astype(jnp.bfloat16)
        t = jnp.concatenate(parts, axis=0).T
        for p in range(pack):
            cols = slice(p * seqs, (p + 1) * seqs)
            for which in range(2):
                base = which * hidden
                z = jnp.concatenate([t[base : base + half, cols], t[base + half : base + hidden, cols]], axis=1)
                turned[which, (i + p) * half : (i + p + 1) * half, :] = z
    for r in range(half):
        lanes = slice(r * LANES, (r + 1) * LANES)
        for which in range(2):
            z = turned[which, pl.ds(r, rows, stride=half), :].astype(jnp.bfloat16)
            flat_ref[which * rows : (which + 1) * rows, lanes] = z
    for c in others:
        c.wait()
    for k in range(n):
        at = pl.multiple_of((me ^ k) * rows, rows)
        (mine_ref, theirs_ref)[k % 2][k // 2] = pair_ref[:, pl.ds(at, rows), :]


def project(n, x, pair, g, b, w1, c1, w2, c2, w):
    seqs, rows, depth = x.shape
    width = pair.shape[2]
    hidden = w1.shape[0]
    flat = jax.ShapeDtypeStruct((2 * rows, hidden * seqs), jnp.bfloat16)
    return pl.pallas_call(
        functools.partial(_project_kernel, n),
        in_specs=[ANY] * 9,
        out_specs=(VMEM,) * 5,
        out_shape=(jax.ShapeDtypeStruct((rows, seqs, 2 * hidden), jnp.bfloat16), flat, jax.ShapeDtypeStruct(w.shape, w.dtype))
        + (jax.ShapeDtypeStruct((n // 2, rows, rows, width), jnp.bfloat16),) * 2,
        scratch_shapes=[
            pltpu.VMEM(x.shape, x.dtype),
            pltpu.VMEM(pair.shape, pair.dtype),
            pltpu.VMEM(g.shape, g.dtype),
            pltpu.VMEM(b.shape, b.dtype),
            pltpu.VMEM((2 * hidden, depth), w1.dtype),
            pltpu.VMEM((2,) + c1.shape, c1.dtype),
            pltpu.VMEM((seqs * rows, LANES), jnp.float32),
            pltpu.VMEM((2, rows * hidden // 2, LANES), jnp.float32),
            pltpu.SemaphoreType.DMA((6,)),
            pltpu.SemaphoreType.DMA((2,)),
            pltpu.SemaphoreType.DMA((2,)),
        ],
        compiler_params=pltpu.CompilerParams(vmem_limit_bytes=56 * MIB),
        cost_estimate=_cost(2_000_000_000, 3_000_000),
        name="project",
    )(x, pair, g, b, w1, c1, w2, c2, w)


def _spread_kernel(which, local_ref, w_ref, *refs):
    out_ref, wf = refs
    rows, seqs, both = local_ref.shape
    hidden = both // 2
    half = hidden // 2
    width = w_ref.shape[1]
    wf[...] = w_ref[...].astype(jnp.float32)
    blank = jnp.zeros((hidden, 2 * width), jnp.float32)
    group = 256 // seqs

    def weights(r):
        if which == 0:
            return wf[pl.ds(r, hidden, stride=hidden), :]
        return wf[r * hidden : (r + 1) * hidden, :]

    for r in range(half):
        wr = jnp.concatenate([weights(r), weights(r + half)], axis=1)
        wr = jnp.concatenate([wr, blank] if which == 0 else [blank, wr], axis=0).astype(jnp.bfloat16)
        for i in range(0, rows, group):
            a = local_ref[i : i + group].reshape(group * seqs, both)
            y = jnp.dot(a, wr, preferred_element_type=jnp.float32).astype(jnp.bfloat16)
            for k in range(group):
                for h in range(2):
                    out_ref[
                        (i + k) // 2,
                        (2 * r + h) * seqs : (2 * r + h + 1) * seqs,
                        (k % 2) * width : (k % 2 + 1) * width,
                    ] = y[k * seqs : (k + 1) * seqs, h * width : (h + 1) * width]


def spread_weights(which, local, w):
    rows, seqs, both = local.shape
    hidden = both // 2
    width = w.shape[1]
    return pl.pallas_call(
        functools.partial(_spread_kernel, which),
        in_specs=[VMEM, VMEM],
        out_specs=VMEM,
        out_shape=pltpu.VMEM((rows // 2, hidden * seqs, 2 * width), jnp.bfloat16),
        scratch_shapes=[pltpu.VMEM(w.shape, jnp.float32)],
        compiler_params=pltpu.CompilerParams(vmem_limit_bytes=8 * MIB),
        cost_estimate=_cost(2_500_000_000, 1_000_000),
        name=("spread_first", "spread_second")[which],
    )(local, w)


def _update_kernel(order, scale, bias_ref, pair_ref, t_ref, u_ref, *refs):
    pieces = refs[: len(order)]
    out_ref, late_ref, seconds, firsts, pair, pair_sem, out_sem = refs[len(order) :]
    rows, _, width = pair.shape
    fetch = pltpu.make_async_copy(pair_ref, pair, pair_sem)
    fetch.start()
    me = lax.axis_index("row")
    for ks, piece in zip(order, pieces):
        for n, k in enumerate(ks):
            at = pl.multiple_of((me ^ k) * rows, rows)
            firsts[pl.ds(at, rows), :] = piece[2 * n * rows : (2 * n + 1) * rows, :]
            seconds[pl.ds(at, rows), :] = piece[(2 * n + 1) * rows : (2 * n + 2) * rows, :]
    fetch.wait()
    sends = []
    step = min(256, pair.shape[1])

    def spans(f):
        if pair.shape[1] == step:
            f(slice(None))
        else:
            pl.loop(0, pair.shape[1] // step)(lambda c: f(pl.ds(pl.multiple_of(c * step, step), step)))

    for i in range(rows // 2):

        def early(c):
            y = jnp.dot(seconds[c, :], t_ref[i], preferred_element_type=jnp.float32)
            for k in range(2):
                up = y[:, k * width : (k + 1) * width] * scale + bias_ref[...]
                pair[2 * i + k, c, :] = (pair[2 * i + k, c, :].astype(jnp.float32) + up).astype(jnp.bfloat16)

        spans(early)
        sends.append(pltpu.make_async_copy(pair.at[pl.ds(2 * i, 2)], out_ref.at[pl.ds(2 * i, 2)], out_sem.at[i]))
        sends[-1].start()
    for i in range(rows // 2):

        def later(c):
            y = jnp.dot(firsts[c, :], u_ref[i], preferred_element_type=jnp.float32)
            for k in range(2):
                late_ref[2 * i + k, c, :] = y[:, k * width : (k + 1) * width] * scale + bias_ref[...]

        spans(later)
    for c in sends:
        c.wait()


def update(order, scale, bias, pair, t, u, pieces):
    span, inner = pair.shape[1], pieces[0].shape[1]
    rows = pair.shape[0]
    return pl.pallas_call(
        functools.partial(_update_kernel, order, scale),
        in_specs=[VMEM, ANY, VMEM, VMEM] + [VMEM] * len(order),
        out_specs=(ANY, VMEM),
        out_shape=(
            jax.ShapeDtypeStruct(pair.shape, jnp.bfloat16),
            jax.ShapeDtypeStruct(pair.shape, jnp.float32),
        ),
        scratch_shapes=[
            pltpu.VMEM((span, inner), jnp.bfloat16),
            pltpu.VMEM((span, inner), jnp.bfloat16),
            pltpu.VMEM(pair.shape, jnp.bfloat16),
            pltpu.SemaphoreType.DMA,
            pltpu.SemaphoreType.DMA((rows // 2,)),
        ],
        compiler_params=pltpu.CompilerParams(vmem_limit_bytes=(8 + 4 * span // 256) * MIB),
        cost_estimate=_cost(5_000_000_000, 6_000_000),
        name="update",
    )(bias, pair, t, u, *pieces)


def _add_kernel(order, late_ref, *refs):
    got = refs[: len(order)]
    out_hbm, staged, out_sem = refs[len(order) :]
    _, rows, _, width = got[0].shape
    n = rows * rows
    shift = rows.bit_length() - 1
    me = lax.axis_index("row")
    a = lax.broadcasted_iota(jnp.int32, (n, n), 0)
    b = lax.broadcasted_iota(jnp.int32, (n, n), 1)
    turn = jnp.where(((a & (rows - 1)) << shift) + (a >> shift) == b, 1.0, 0.0).astype(jnp.bfloat16)
    sends = []
    for c, piece in zip(order, got):
        z = jnp.concatenate([piece[0].reshape(n, width), piece[1].reshape(n, width)], axis=1)
        y = jnp.dot(turn, z, preferred_element_type=jnp.float32)
        for k in range(2):
            part = pl.ds(pl.multiple_of((me ^ c ^ k) * rows, rows), rows)
            up = y[:, k * width : (k + 1) * width].reshape(rows, rows, width)
            staged[:, part, :] = (up + late_ref[:, part, :]).astype(jnp.bfloat16)
            sends.append(pltpu.make_async_copy(staged.at[:, part, :], out_hbm.at[:, part, :], out_sem.at[c + k]))
            sends[-1].start()
    for x in sends:
        x.wait()


def add_turned(order, got, late):
    return pl.pallas_call(
        functools.partial(_add_kernel, order),
        in_specs=[VMEM] * (1 + len(order)),
        out_specs=ANY,
        out_shape=jax.ShapeDtypeStruct(late.shape, jnp.bfloat16),
        scratch_shapes=[pltpu.VMEM(late.shape, jnp.bfloat16), pltpu.SemaphoreType.DMA((2 * len(order),))],
        compiler_params=pltpu.CompilerParams(vmem_limit_bytes=24 * MIB),
        cost_estimate=_cost(500_000_000, 4_000_000),
        name="add_turned",
    )(late, *got)


def _pack_kernel(a_ref, b_ref, out_ref):
    out_ref[: a_ref.shape[0], :] = a_ref[...]
    out_ref[a_ref.shape[0] :, :] = b_ref[...]


def pack(a, b):
    return pl.pallas_call(
        _pack_kernel,
        in_specs=[VMEM, VMEM],
        out_specs=VMEM,
        out_shape=jax.ShapeDtypeStruct((a.shape[0] + b.shape[0], a.shape[1]), a.dtype),
        compiler_params=pltpu.CompilerParams(vmem_limit_bytes=4 * MIB),
        cost_estimate=_cost(0, 4 * a.size),
        name="pack",
    )(a, b)


def _pair_up_kernel(mine_ref, theirs_ref, *out_refs):
    for q, out_ref in enumerate(out_refs):
        out_ref[0] = mine_ref[q]
        out_ref[1] = theirs_ref[q]


def pair_up(mine, theirs):
    return pl.pallas_call(
        _pair_up_kernel,
        in_specs=[VMEM, VMEM],
        out_specs=(VMEM,) * mine.shape[0],
        out_shape=(jax.ShapeDtypeStruct((2,) + mine.shape[1:], mine.dtype),) * mine.shape[0],
        compiler_params=pltpu.CompilerParams(vmem_limit_bytes=4 * MIB),
        cost_estimate=_cost(0, 4 * mine.size),
        name="pair_up",
    )(mine, theirs)


def tie(x, *after):
    return lax.optimization_barrier((x,) + after)[0] if after else x


def swap(x, k, n):
    return lax.ppermute(x, "row", [(i, i ^ k) for i in range(n)])


def schedule(n):
    gathers, order, k = [], [0], n // 4
    while k:
        gathers += [(True, k, o) for o in order]
        order += [o ^ k for o in order]
        k //= 2
    gathers.sort(key=lambda g: (g[2].bit_count(), -g[1], g[2]))
    far = [(False, k, 0) for q in (0, 2) for k in range(n // 2 + q, n, 4)]
    near = [(False, k, 0) for q in (0, 2) for k in range(4 - q, n // 2, 4)]
    levels = n.bit_length() - 2
    rest = []
    for level in range(levels):
        rest += [g for g in gathers if g[2].bit_count() == level]
        rest += near[level * len(near) // levels : (level + 1) * len(near) // levels]
    plan = []
    for at, op in enumerate(far):
        plan.append(op)
        plan += rest[at * len(rest) // len(far) : (at + 1) * len(rest) // len(far)]
    return plan, tuple(order)


DEPTH = 5


def body(n, x, pair, g, b, w1, b1, w2, b2, w, bias):
    seqs, rows, depth = x.shape
    width = pair.shape[-1]
    hidden = w1.shape[1]
    local, flat, w, mine, theirs = project(
        n, x, pair, g.reshape(1, depth), b.reshape(1, depth),
        w1.T, b1.reshape(1, hidden), w2.T, b2.reshape(1, hidden), w,
    )
    far = swap(flat, n // 2, n)
    blocks = pair_up(mine, swap(theirs, 1, n))
    t = spread_weights(0, local, w)
    pieces, got, done = {0: pack(flat, tie(far, t))}, {0: blocks[0]}, [far, far]
    u = None
    plan, order = schedule(n)
    for at, (gathering, k, o) in enumerate(plan, len(done)):
        after = done[max(at - DEPTH - 4, 0) : max(at - DEPTH + 1, 0)]
        source = pieces[o] if gathering else blocks[k // 2]
        if at == DEPTH + 2:
            u = spread_weights(1, tie(local, *after[-1:]), w)
        if u is not None:
            after = after + [u]
        result = swap(tie(source, *after), k, n)
        done.append(result)
        if gathering:
            pieces[o ^ k] = result
        else:
            got[k] = result
    scale = 1.0 / seqs
    bias = bias.reshape(1, width)
    places = tuple((o, o ^ (n // 2)) for o in order)
    pair_rows, late = update(places, scale, bias, pair, t, u, [pieces[o] for o in order])
    chips = tuple(range(0, n, 2))
    return pair_rows, add_turned(chips, [got[k] for k in chips], late)


def solution(mesh):
    pair_spec = P(("grp", "row"), None, None)
    in_specs = (P("grp", "row", None), pair_spec) + (P(),) * 8
    return jax.shard_map(
        functools.partial(body, mesh.shape["row"]),
        mesh=mesh,
        in_specs=in_specs,
        out_specs=(pair_spec, pair_spec),
        check_vma=False,
    )
```

```python
import functools

import jax
import jax.numpy as jnp
from jax import lax
from jax.experimental import pallas as pl
from jax.experimental.pallas import tpu as pltpu
from jax.sharding import PartitionSpec as P

LANES = 128
MIB = 1 << 20
ANY = pl.BlockSpec(memory_space=pl.ANY)
VMEM = pl.BlockSpec(memory_space=pltpu.VMEM)
SMEM = pl.BlockSpec(memory_space=pltpu.SMEM)


def _cost(flops, nbytes):
    return pl.CostEstimate(flops=0, bytes_accessed=0, transcendentals=0)


def _project_kernel(
    n, x_hbm, pair_hbm, g_hbm, b_hbm, w1_hbm, c1_hbm, w2_hbm, c2_hbm, w_hbm, local_ref, flat_ref, out_w_ref, mine_ref, theirs_ref, *refs
):
    x_ref, pair_ref, g_ref, b_ref, w_ref, c_ref, proj, turned, in_sem, x_sem, sem = refs
    me = lax.axis_index("row")
    seqs, rows, depth = x_ref.shape
    hidden = w_ref.shape[0] // 2
    half = hidden // 2
    step = 8
    loads = [
        pltpu.make_async_copy(src, dst, in_sem.at[k])
        for k, (src, dst) in enumerate(
            (
                (g_hbm, g_ref),
                (b_hbm, b_ref),
                (w1_hbm, w_ref.at[pl.ds(0, hidden), :]),
                (w2_hbm, w_ref.at[pl.ds(hidden, hidden), :]),
                (c1_hbm, c_ref.at[0]),
                (c2_hbm, c_ref.at[1]),
            )
        )
    ]
    part = seqs // 2
    chunks = [
        pltpu.make_async_copy(x_hbm.at[pl.ds(k * part, part)], x_ref.at[pl.ds(k * part, part)], x_sem.at[k])
        for k in range(2)
    ]
    others = [pltpu.make_async_copy(pair_hbm, pair_ref, sem.at[0]), pltpu.make_async_copy(w_hbm, out_w_ref, sem.at[1])]
    for c in chunks[:1] + loads + chunks[1:] + others:
        c.start()
    for c in loads:
        c.wait()
    bias = jnp.concatenate([c_ref[0], c_ref[1]], axis=1)
    for s in range(0, seqs, step):
        if s % part == 0:
            chunks[s // part].wait()
        x = x_ref[s : s + step].astype(jnp.float32).reshape(step * rows, depth)
        center = jnp.mean(x, axis=-1, keepdims=True)
        x = x - center
        spread = jnp.mean(x * x, axis=-1, keepdims=True)
        normed = (x * lax.rsqrt(spread + 1e-05) * g_ref[...] + b_ref[...]).astype(jnp.bfloat16)
        y = lax.dot_general(normed, w_ref[...], (((1,), (1,)), ((), ())), preferred_element_type=jnp.float32)
        y = (y + bias).astype(jnp.bfloat16).astype(jnp.float32)
        proj[s * rows : (s + step) * rows, :] = jnp.concatenate(
            [y, jnp.zeros((step * rows, LANES - 2 * hidden), jnp.float32)], axis=1
        )
    pack = LANES // seqs
    for i in range(0, rows, pack):
        parts = [proj[pl.ds(i + p, seqs, stride=rows), :] for p in range(pack)]
        for p in range(pack):
            local_ref[i + p] = parts[p][:, : 2 * hidden].astype(jnp.bfloat16)
        t = jnp.concatenate(parts, axis=0).T
        for p in range(pack):
            cols = slice(p * seqs, (p + 1) * seqs)
            for which in range(2):
                base = which * hidden
                z = jnp.concatenate([t[base : base + half, cols], t[base + half : base + hidden, cols]], axis=1)
                turned[which, (i + p) * half : (i + p + 1) * half, :] = z
    for r in range(half):
        lanes = slice(r * LANES, (r + 1) * LANES)
        for which in range(2):
            z = turned[which, pl.ds(r, rows, stride=half), :].astype(jnp.bfloat16)
            flat_ref[which * rows : (which + 1) * rows, lanes] = z
    for c in others:
        c.wait()
    for k in range(n):
        at = pl.multiple_of((me ^ k) * rows, rows)
        (mine_ref, theirs_ref)[k % 2][k // 2] = pair_ref[:, pl.ds(at, rows), :]


def project(n, x, pair, g, b, w1, c1, w2, c2, w):
    seqs, rows, depth = x.shape
    width = pair.shape[2]
    hidden = w1.shape[0]
    return pl.pallas_call(
        functools.partial(_project_kernel, n),
        in_specs=[ANY] * 9,
        out_specs=(VMEM,) * 5,
        out_shape=(
            pltpu.VMEM((rows, seqs, 2 * hidden), jnp.bfloat16),
            pltpu.VMEM((2 * rows, hidden * seqs), jnp.bfloat16),
            pltpu.VMEM(w.shape, w.dtype),
            pltpu.VMEM((n // 2, rows, rows, width), jnp.bfloat16),
            pltpu.VMEM((n // 2, rows, rows, width), jnp.bfloat16),
        ),
        scratch_shapes=[
            pltpu.VMEM(x.shape, x.dtype),
            pltpu.VMEM(pair.shape, pair.dtype),
            pltpu.VMEM(g.shape, g.dtype),
            pltpu.VMEM(b.shape, b.dtype),
            pltpu.VMEM((2 * hidden, depth), w1.dtype),
            pltpu.VMEM((2,) + c1.shape, c1.dtype),
            pltpu.VMEM((seqs * rows, LANES), jnp.float32),
            pltpu.VMEM((2, rows * hidden // 2, LANES), jnp.float32),
            pltpu.SemaphoreType.DMA((6,)),
            pltpu.SemaphoreType.DMA((2,)),
            pltpu.SemaphoreType.DMA((2,)),
        ],
        compiler_params=pltpu.CompilerParams(vmem_limit_bytes=56 * MIB),
        cost_estimate=_cost(2_000_000_000, 3_000_000),
        name="project",
    )(x, pair, g, b, w1, c1, w2, c2, w)


def _spread_kernel(which, local_ref, w_ref, *refs):
    out_ref, wf = refs
    rows, seqs, both = local_ref.shape
    hidden = both // 2
    half = hidden // 2
    width = w_ref.shape[1]
    wf[...] = w_ref[...].astype(jnp.float32)
    blank = jnp.zeros((hidden, 2 * width), jnp.float32)
    group = 256 // seqs

    def weights(r):
        if which == 0:
            return wf[pl.ds(r, hidden, stride=hidden), :]
        return wf[r * hidden : (r + 1) * hidden, :]

    for r in range(half):
        wr = jnp.concatenate([weights(r), weights(r + half)], axis=1)
        wr = jnp.concatenate([wr, blank] if which == 0 else [blank, wr], axis=0).astype(jnp.bfloat16)
        for i in range(0, rows, group):
            a = local_ref[i : i + group].reshape(group * seqs, both)
            y = jnp.dot(a, wr, preferred_element_type=jnp.float32).astype(jnp.bfloat16)
            for k in range(group):
                for h in range(2):
                    out_ref[
                        (i + k) // 2,
                        (2 * r + h) * seqs : (2 * r + h + 1) * seqs,
                        (k % 2) * width : (k % 2 + 1) * width,
                    ] = y[k * seqs : (k + 1) * seqs, h * width : (h + 1) * width]


def spread_weights(which, local, w):
    rows, seqs, both = local.shape
    hidden = both // 2
    width = w.shape[1]
    return pl.pallas_call(
        functools.partial(_spread_kernel, which),
        in_specs=[VMEM, VMEM],
        out_specs=VMEM,
        out_shape=pltpu.VMEM((rows // 2, hidden * seqs, 2 * width), jnp.bfloat16),
        scratch_shapes=[pltpu.VMEM(w.shape, jnp.float32)],
        compiler_params=pltpu.CompilerParams(vmem_limit_bytes=8 * MIB),
        cost_estimate=_cost(2_500_000_000, 1_000_000),
        name=("spread_first", "spread_second")[which],
    )(local, w)


def _update_kernel(order, scale, bias_ref, pair_ref, t_ref, u_ref, *refs):
    pieces = refs[: len(order)]
    out_ref, late_ref, seconds, firsts, pair, pair_sem, out_sem = refs[len(order) :]
    rows, _, width = pair.shape
    fetch = pltpu.make_async_copy(pair_ref, pair, pair_sem)
    fetch.start()
    me = lax.axis_index("row")
    for ks, piece in zip(order, pieces):
        for n, k in enumerate(ks):
            at = pl.multiple_of((me ^ k) * rows, rows)
            firsts[pl.ds(at, rows), :] = piece[2 * n * rows : (2 * n + 1) * rows, :]
            seconds[pl.ds(at, rows), :] = piece[(2 * n + 1) * rows : (2 * n + 2) * rows, :]
    fetch.wait()
    sends = []
    step = min(256, pair.shape[1])

    def spans(f):
        if pair.shape[1] == step:
            f(slice(None))
        else:
            pl.loop(0, pair.shape[1] // step)(lambda c: f(pl.ds(pl.multiple_of(c * step, step), step)))

    for i in range(rows // 2):

        def early(c):
            y = jnp.dot(seconds[c, :], t_ref[i], preferred_element_type=jnp.float32)
            for k in range(2):
                up = y[:, k * width : (k + 1) * width] * scale + bias_ref[...]
                pair[2 * i + k, c, :] = (pair[2 * i + k, c, :].astype(jnp.float32) + up).astype(jnp.bfloat16)

        spans(early)
        sends.append(pltpu.make_async_copy(pair.at[pl.ds(2 * i, 2)], out_ref.at[pl.ds(2 * i, 2)], out_sem.at[i]))
        sends[-1].start()
    for i in range(rows // 2):

        def later(c):
            y = jnp.dot(firsts[c, :], u_ref[i], preferred_element_type=jnp.float32)
            for k in range(2):
                late_ref[2 * i + k, c, :] = y[:, k * width : (k + 1) * width] * scale + bias_ref[...]

        spans(later)
    for c in sends:
        c.wait()


def update(order, scale, bias, pair, t, u, pieces):
    span, inner = pair.shape[1], pieces[0].shape[1]
    rows = pair.shape[0]
    return pl.pallas_call(
        functools.partial(_update_kernel, order, scale),
        in_specs=[VMEM, ANY, VMEM, VMEM] + [VMEM] * len(order),
        out_specs=(ANY, VMEM),
        out_shape=(
            jax.ShapeDtypeStruct(pair.shape, jnp.bfloat16),
            jax.ShapeDtypeStruct(pair.shape, jnp.float32),
        ),
        scratch_shapes=[
            pltpu.VMEM((span, inner), jnp.bfloat16),
            pltpu.VMEM((span, inner), jnp.bfloat16),
            pltpu.VMEM(pair.shape, jnp.bfloat16),
            pltpu.SemaphoreType.DMA,
            pltpu.SemaphoreType.DMA((rows // 2,)),
        ],
        compiler_params=pltpu.CompilerParams(vmem_limit_bytes=(8 + 4 * span // 256) * MIB),
        cost_estimate=_cost(0, 0),
        name="update",
    )(bias, pair, t, u, *pieces)


def _add_kernel(order, late_ref, *refs):
    got = refs[: len(order)]
    out_hbm, staged, out_sem = refs[len(order) :]
    _, rows, _, width = got[0].shape
    n = rows * rows
    shift = rows.bit_length() - 1
    me = lax.axis_index("row")
    a = lax.broadcasted_iota(jnp.int32, (n, n), 0)
    b = lax.broadcasted_iota(jnp.int32, (n, n), 1)
    turn = jnp.where(((a & (rows - 1)) << shift) + (a >> shift) == b, 1.0, 0.0).astype(jnp.bfloat16)
    sends = []
    for c, piece in zip(order, got):
        z = jnp.concatenate([piece[0].reshape(n, width), piece[1].reshape(n, width)], axis=1)
        y = jnp.dot(turn, z, preferred_element_type=jnp.float32)
        for k in range(2):
            part = pl.ds(pl.multiple_of((me ^ c ^ k) * rows, rows), rows)
            up = y[:, k * width : (k + 1) * width].reshape(rows, rows, width)
            staged[:, part, :] = (up + late_ref[:, part, :]).astype(jnp.bfloat16)
            sends.append(pltpu.make_async_copy(staged.at[:, part, :], out_hbm.at[:, part, :], out_sem.at[c + k]))
            sends[-1].start()
    for x in sends:
        x.wait()


def add_turned(order, got, late):
    return pl.pallas_call(
        functools.partial(_add_kernel, order),
        in_specs=[VMEM] * (1 + len(order)),
        out_specs=ANY,
        out_shape=jax.ShapeDtypeStruct(late.shape, jnp.bfloat16),
        scratch_shapes=[pltpu.VMEM(late.shape, jnp.bfloat16), pltpu.SemaphoreType.DMA((2 * len(order),))],
        compiler_params=pltpu.CompilerParams(vmem_limit_bytes=24 * MIB),
        cost_estimate=_cost(500_000_000, 4_000_000),
        name="add_turned",
    )(late, *got)


def _pack_kernel(*refs):
    rows = refs[0].shape[0]
    for k, ref in enumerate(refs[:-1]):
        refs[-1][k * rows : (k + 1) * rows, :] = ref[...]


def pack(pieces):
    rows, inner = pieces[0].shape
    return pl.pallas_call(
        _pack_kernel,
        in_specs=[VMEM] * len(pieces),
        out_specs=VMEM,
        out_shape=pltpu.VMEM((rows * len(pieces), inner), pieces[0].dtype),
        compiler_params=pltpu.CompilerParams(vmem_limit_bytes=4 * MIB),
        cost_estimate=_cost(0, 0),
        name="pack",
    )(*pieces)


def _pair_up_kernel(mine_ref, theirs_ref, *out_refs):
    for q, out_ref in enumerate(out_refs):
        out_ref[0] = mine_ref[q]
        out_ref[1] = theirs_ref[q]


def pair_up(mine, theirs):
    return pl.pallas_call(
        _pair_up_kernel,
        in_specs=[VMEM, VMEM],
        out_specs=(VMEM,) * mine.shape[0],
        out_shape=(jax.ShapeDtypeStruct((2,) + mine.shape[1:], mine.dtype),) * mine.shape[0],
        compiler_params=pltpu.CompilerParams(vmem_limit_bytes=4 * MIB),
        cost_estimate=_cost(0, 4 * mine.size),
        name="pair_up",
    )(mine, theirs)


def tie(x, *after):
    return lax.optimization_barrier((x,) + after)[0] if after else x


def swap(x, k, n):
    return lax.ppermute(x, "row", [(i, i ^ k) for i in range(n)])


TIES = {
    16: {
        "E10": ("E12",),
        "E14": ("E8",),
        "E2": ("G4_8",),
        "E4": ("G4_8",),
        "E6": ("G2_12",),
        "E8": ("G8_0",),
        "G2_12": ("E12", "T"),
        "G2_4": ("E12", "G2_0"),
        "T": ("G4_0",),
        "U": ("G4_8",),
        "Y0": ("E8",),
        "Y2": ("E10", "U"),
    }
}


def waits(n):
    if n in TIES:
        return TIES[n]
    far = [f"E{k}" for k in range(n // 2, n, 2)]
    near = [f"E{k}" for k in range(2, n // 2, 2)]
    after = {"T": (f"G{n // 4}_0",), "Y2": ("U",), "U": ("T",), far[0]: (f"G{n // 2}_0",), far[1]: (f"G{n // 2}_0",)}
    after.update({b: (a,) for a, b in zip(far, far[2:])})
    after.update({b: (a,) for a, b in zip(far, near)})
    return after


def body(n, x, pair, g, b, w1, b1, w2, b2, w, bias):
    seqs, rows, depth = x.shape
    width = pair.shape[-1]
    hidden = w1.shape[1]
    local, flat, w, mine, theirs = project(
        n, x, pair, g.reshape(1, depth), b.reshape(1, depth),
        w1.T, b1.reshape(1, hidden), w2.T, b2.reshape(1, hidden), w,
    )
    after, done = waits(n), {}
    halves = {h: tuple(o for o in range(0, n, 2) if o & 2 == h) for h in (0, 2)}

    def need(name):
        if name not in done:
            done[name] = make(name)
        return done[name]

    def held(x, name):
        return tie(x, *[need(k) for k in after.get(name, ())])

    def piece(o):
        return need(f"G{o & -o}_{o & (o - 1)}") if o else flat

    def make(name):
        if name == "X":
            return swap(theirs, 1, n)
        if name == "B":
            return pair_up(mine, need("X"))
        if name in ("T", "U"):
            return spread_weights("TU".index(name), held(local, name), w)
        if name[0] == "P":
            return pack([piece(o) for o in halves[int(name[1:])]])
        if name[0] == "Y":
            return swap(held(need("P" + name[1:]), name), 1, n)
        if name[0] == "E":
            k = int(name[1:])
            return swap(held(need("B")[k // 2], name), k, n)
        k, o = map(int, name[1:].split("_"))
        return swap(held(piece(o), name), k, n)

    pieces = [need(f"{a}{h}") for h in halves for a in "PY"]
    places = [tuple(o ^ q for o in halves[h]) for h in halves for q in (0, 1)]
    scale = 1.0 / seqs
    bias = bias.reshape(1, width)
    pair_rows, late = update(places, scale, bias, held(pair, "K"), need("T"), need("U"), pieces)
    chips = tuple(range(0, n, 2))
    return pair_rows, add_turned(chips, [need(f"E{k}") if k else need("B")[0] for k in chips], late)


def solution(mesh):
    pair_spec = P(("grp", "row"), None, None)
    in_specs = (P("grp", "row", None), pair_spec) + (P(),) * 8
    return jax.shard_map(
        functools.partial(body, mesh.shape["row"]),
        mesh=mesh,
        in_specs=in_specs,
        out_specs=(pair_spec, pair_spec),
        check_vma=False,
    )
```

```python
import functools

import jax
import jax.numpy as jnp
from jax import lax
from jax.experimental import pallas as pl
from jax.experimental.pallas import tpu as pltpu
from jax.sharding import PartitionSpec as P

LANES = 128
MIB = 1 << 20
ANY = pl.BlockSpec(memory_space=pl.ANY)
VMEM = pl.BlockSpec(memory_space=pltpu.VMEM)
SMEM = pl.BlockSpec(memory_space=pltpu.SMEM)


def _cost(flops, nbytes):
    return pl.CostEstimate(flops=0, bytes_accessed=0, transcendentals=0)


def _project_kernel(
    n, x_hbm, pair_hbm, g_hbm, b_hbm, w1_hbm, c1_hbm, w2_hbm, c2_hbm, w_hbm, local_ref, flat_ref, out_w_ref, mine_ref, theirs_ref, *refs
):
    x_ref, pair_ref, g_ref, b_ref, w_ref, c_ref, proj, turned, in_sem, x_sem, sem = refs
    me = lax.axis_index("row")
    seqs, rows, depth = x_ref.shape
    hidden = w_ref.shape[0] // 2
    half = hidden // 2
    step = 8
    loads = [
        pltpu.make_async_copy(src, dst, in_sem.at[k])
        for k, (src, dst) in enumerate(
            (
                (g_hbm, g_ref),
                (b_hbm, b_ref),
                (w1_hbm, w_ref.at[pl.ds(0, hidden), :]),
                (w2_hbm, w_ref.at[pl.ds(hidden, hidden), :]),
                (c1_hbm, c_ref.at[0]),
                (c2_hbm, c_ref.at[1]),
            )
        )
    ]
    part = seqs // 2
    chunks = [
        pltpu.make_async_copy(x_hbm.at[pl.ds(k * part, part)], x_ref.at[pl.ds(k * part, part)], x_sem.at[k])
        for k in range(2)
    ]
    others = [pltpu.make_async_copy(pair_hbm, pair_ref, sem.at[0]), pltpu.make_async_copy(w_hbm, out_w_ref, sem.at[1])]
    for c in chunks[:1] + loads + chunks[1:] + others:
        c.start()
    for c in loads:
        c.wait()
    bias = jnp.concatenate([c_ref[0], c_ref[1]], axis=1)
    for s in range(0, seqs, step):
        if s % part == 0:
            chunks[s // part].wait()
        x = x_ref[s : s + step].astype(jnp.float32).reshape(step * rows, depth)
        center = jnp.mean(x, axis=-1, keepdims=True)
        x = x - center
        spread = jnp.mean(x * x, axis=-1, keepdims=True)
        normed = (x * lax.rsqrt(spread + 1e-05) * g_ref[...] + b_ref[...]).astype(jnp.bfloat16)
        y = lax.dot_general(normed, w_ref[...], (((1,), (1,)), ((), ())), preferred_element_type=jnp.float32)
        y = (y + bias).astype(jnp.bfloat16).astype(jnp.float32)
        proj[s * rows : (s + step) * rows, :] = jnp.concatenate(
            [y, jnp.zeros((step * rows, LANES - 2 * hidden), jnp.float32)], axis=1
        )
    pack = LANES // seqs
    for i in range(0, rows, pack):
        parts = [proj[pl.ds(i + p, seqs, stride=rows), :] for p in range(pack)]
        for p in range(pack):
            local_ref[i + p] = parts[p][:, : 2 * hidden].astype(jnp.bfloat16)
        t = jnp.concatenate(parts, axis=0).T
        for p in range(pack):
            cols = slice(p * seqs, (p + 1) * seqs)
            for which in range(2):
                base = which * hidden
                z = jnp.concatenate([t[base : base + half, cols], t[base + half : base + hidden, cols]], axis=1)
                turned[which, (i + p) * half : (i + p + 1) * half, :] = z
    for r in range(half):
        lanes = slice(r * LANES, (r + 1) * LANES)
        for which in range(2):
            z = turned[which, pl.ds(r, rows, stride=half), :].astype(jnp.bfloat16)
            flat_ref[which * rows : (which + 1) * rows, lanes] = z
    for c in others:
        c.wait()
    for k in range(n):
        at = pl.multiple_of((me ^ k) * rows, rows)
        (mine_ref, theirs_ref)[k % 2][k // 2] = pair_ref[:, pl.ds(at, rows), :]


def project(n, x, pair, g, b, w1, c1, w2, c2, w):
    seqs, rows, depth = x.shape
    width = pair.shape[2]
    hidden = w1.shape[0]
    return pl.pallas_call(
        functools.partial(_project_kernel, n),
        in_specs=[ANY] * 9,
        out_specs=(VMEM,) * 5,
        out_shape=(
            pltpu.VMEM((rows, seqs, 2 * hidden), jnp.bfloat16),
            pltpu.VMEM((2 * rows, hidden * seqs), jnp.bfloat16),
            pltpu.VMEM(w.shape, w.dtype),
            pltpu.VMEM((n // 2, rows, rows, width), jnp.bfloat16),
            pltpu.VMEM((n // 2, rows, rows, width), jnp.bfloat16),
        ),
        scratch_shapes=[
            pltpu.VMEM(x.shape, x.dtype),
            pltpu.VMEM(pair.shape, pair.dtype),
            pltpu.VMEM(g.shape, g.dtype),
            pltpu.VMEM(b.shape, b.dtype),
            pltpu.VMEM((2 * hidden, depth), w1.dtype),
            pltpu.VMEM((2,) + c1.shape, c1.dtype),
            pltpu.VMEM((seqs * rows, LANES), jnp.float32),
            pltpu.VMEM((2, rows * hidden // 2, LANES), jnp.float32),
            pltpu.SemaphoreType.DMA((6,)),
            pltpu.SemaphoreType.DMA((2,)),
            pltpu.SemaphoreType.DMA((2,)),
        ],
        compiler_params=pltpu.CompilerParams(vmem_limit_bytes=56 * MIB),
        cost_estimate=_cost(2_000_000_000, 3_000_000),
        name="project",
    )(x, pair, g, b, w1, c1, w2, c2, w)


def _spread_kernel(which, local_ref, w_ref, *refs):
    out_ref, wf = refs
    rows, seqs, both = local_ref.shape
    hidden = both // 2
    half = hidden // 2
    width = w_ref.shape[1]
    wf[...] = w_ref[...].astype(jnp.float32)
    blank = jnp.zeros((hidden, 2 * width), jnp.float32)
    group = 256 // seqs

    def weights(r):
        if which == 0:
            return wf[pl.ds(r, hidden, stride=hidden), :]
        return wf[r * hidden : (r + 1) * hidden, :]

    for r in range(half):
        wr = jnp.concatenate([weights(r), weights(r + half)], axis=1)
        wr = jnp.concatenate([wr, blank] if which == 0 else [blank, wr], axis=0).astype(jnp.bfloat16)
        for i in range(0, rows, group):
            a = local_ref[i : i + group].reshape(group * seqs, both)
            y = jnp.dot(a, wr, preferred_element_type=jnp.float32).astype(jnp.bfloat16)
            for k in range(group):
                for h in range(2):
                    out_ref[
                        (i + k) // 2,
                        (2 * r + h) * seqs : (2 * r + h + 1) * seqs,
                        (k % 2) * width : (k % 2 + 1) * width,
                    ] = y[k * seqs : (k + 1) * seqs, h * width : (h + 1) * width]


def spread_weights(which, local, w):
    rows, seqs, both = local.shape
    hidden = both // 2
    width = w.shape[1]
    return pl.pallas_call(
        functools.partial(_spread_kernel, which),
        in_specs=[VMEM, VMEM],
        out_specs=VMEM,
        out_shape=pltpu.VMEM((rows // 2, hidden * seqs, 2 * width), jnp.bfloat16),
        scratch_shapes=[pltpu.VMEM(w.shape, jnp.float32)],
        compiler_params=pltpu.CompilerParams(vmem_limit_bytes=8 * MIB),
        cost_estimate=_cost(2_500_000_000, 1_000_000),
        name=("spread_first", "spread_second")[which],
    )(local, w)


def _update_kernel(order, scale, bias_ref, pair_ref, t_ref, u_ref, *refs):
    pieces = refs[: len(order)]
    out_ref, late_ref, seconds, firsts, pair, pair_sem, out_sem = refs[len(order) :]
    rows, _, width = pair.shape
    fetch = pltpu.make_async_copy(pair_ref, pair, pair_sem)
    fetch.start()
    me = lax.axis_index("row")
    for ks, piece in zip(order, pieces):
        for n, k in enumerate(ks):
            at = pl.multiple_of((me ^ k) * rows, rows)
            firsts[pl.ds(at, rows), :] = piece[2 * n * rows : (2 * n + 1) * rows, :]
            seconds[pl.ds(at, rows), :] = piece[(2 * n + 1) * rows : (2 * n + 2) * rows, :]
    fetch.wait()
    sends = []
    step = min(256, pair.shape[1])

    def spans(f):
        if pair.shape[1] == step:
            f(slice(None))
        else:
            pl.loop(0, pair.shape[1] // step)(lambda c: f(pl.ds(pl.multiple_of(c * step, step), step)))

    for i in range(rows // 2):

        def early(c):
            y = jnp.dot(seconds[c, :], t_ref[i], preferred_element_type=jnp.float32)
            for k in range(2):
                up = y[:, k * width : (k + 1) * width] * scale + bias_ref[...]
                pair[2 * i + k, c, :] = (pair[2 * i + k, c, :].astype(jnp.float32) + up).astype(jnp.bfloat16)

        spans(early)
        sends.append(pltpu.make_async_copy(pair.at[pl.ds(2 * i, 2)], out_ref.at[pl.ds(2 * i, 2)], out_sem.at[i]))
        sends[-1].start()
    for i in range(rows // 2):

        def later(c):
            y = jnp.dot(firsts[c, :], u_ref[i], preferred_element_type=jnp.float32)
            for k in range(2):
                late_ref[2 * i + k, c, :] = y[:, k * width : (k + 1) * width] * scale + bias_ref[...]

        spans(later)
    for c in sends:
        c.wait()


def update(order, scale, bias, pair, t, u, pieces):
    span, inner = pair.shape[1], pieces[0].shape[1]
    rows = pair.shape[0]
    return pl.pallas_call(
        functools.partial(_update_kernel, order, scale),
        in_specs=[VMEM, ANY, VMEM, VMEM] + [VMEM] * len(order),
        out_specs=(ANY, VMEM),
        out_shape=(
            jax.ShapeDtypeStruct(pair.shape, jnp.bfloat16),
            jax.ShapeDtypeStruct(pair.shape, jnp.float32),
        ),
        scratch_shapes=[
            pltpu.VMEM((span, inner), jnp.bfloat16),
            pltpu.VMEM((span, inner), jnp.bfloat16),
            pltpu.VMEM(pair.shape, jnp.bfloat16),
            pltpu.SemaphoreType.DMA,
            pltpu.SemaphoreType.DMA((rows // 2,)),
        ],
        compiler_params=pltpu.CompilerParams(vmem_limit_bytes=(8 + 4 * span // 256) * MIB),
        cost_estimate=_cost(0, 0),
        name="update",
    )(bias, pair, t, u, *pieces)


def _add_kernel(order, late_ref, *refs):
    got = refs[: len(order)]
    out_hbm, staged, out_sem = refs[len(order) :]
    _, rows, _, width = got[0].shape
    n = rows * rows
    shift = rows.bit_length() - 1
    me = lax.axis_index("row")
    a = lax.broadcasted_iota(jnp.int32, (n, n), 0)
    b = lax.broadcasted_iota(jnp.int32, (n, n), 1)
    turn = jnp.where(((a & (rows - 1)) << shift) + (a >> shift) == b, 1.0, 0.0).astype(jnp.bfloat16)
    sends = []
    for c, piece in zip(order, got):
        z = jnp.concatenate([piece[0].reshape(n, width), piece[1].reshape(n, width)], axis=1)
        y = jnp.dot(turn, z, preferred_element_type=jnp.float32)
        for k in range(2):
            part = pl.ds(pl.multiple_of((me ^ c ^ k) * rows, rows), rows)
            up = y[:, k * width : (k + 1) * width].reshape(rows, rows, width)
            staged[:, part, :] = (up + late_ref[:, part, :]).astype(jnp.bfloat16)
            sends.append(pltpu.make_async_copy(staged.at[:, part, :], out_hbm.at[:, part, :], out_sem.at[c + k]))
            sends[-1].start()
    for x in sends:
        x.wait()


def add_turned(order, got, late):
    return pl.pallas_call(
        functools.partial(_add_kernel, order),
        in_specs=[VMEM] * (1 + len(order)),
        out_specs=ANY,
        out_shape=jax.ShapeDtypeStruct(late.shape, jnp.bfloat16),
        scratch_shapes=[pltpu.VMEM(late.shape, jnp.bfloat16), pltpu.SemaphoreType.DMA((2 * len(order),))],
        compiler_params=pltpu.CompilerParams(vmem_limit_bytes=24 * MIB),
        cost_estimate=_cost(500_000_000, 4_000_000),
        name="add_turned",
    )(late, *got)


def _pack_kernel(*refs):
    rows = refs[0].shape[0]
    for k, ref in enumerate(refs[:-1]):
        refs[-1][k * rows : (k + 1) * rows, :] = ref[...]


def pack(pieces):
    rows, inner = pieces[0].shape
    return pl.pallas_call(
        _pack_kernel,
        in_specs=[VMEM] * len(pieces),
        out_specs=VMEM,
        out_shape=pltpu.VMEM((rows * len(pieces), inner), pieces[0].dtype),
        compiler_params=pltpu.CompilerParams(vmem_limit_bytes=4 * MIB),
        cost_estimate=_cost(0, 0),
        name="pack",
    )(*pieces)


def _pair_up_kernel(mine_ref, theirs_ref, *out_refs):
    for q, out_ref in enumerate(out_refs):
        out_ref[0] = mine_ref[q]
        out_ref[1] = theirs_ref[q]


def pair_up(mine, theirs):
    return pl.pallas_call(
        _pair_up_kernel,
        in_specs=[VMEM, VMEM],
        out_specs=(VMEM,) * mine.shape[0],
        out_shape=(jax.ShapeDtypeStruct((2,) + mine.shape[1:], mine.dtype),) * mine.shape[0],
        compiler_params=pltpu.CompilerParams(vmem_limit_bytes=4 * MIB),
        cost_estimate=_cost(0, 4 * mine.size),
        name="pair_up",
    )(mine, theirs)


def tie(x, *after):
    return lax.optimization_barrier((x,) + after)[0] if after else x


def swap(x, k, n):
    return lax.ppermute(x, "row", [(i, i ^ k) for i in range(n)])


TIES = {
    16: {
        "E10": ("E12",),
        "E14": ("E8",),
        "E2": ("G4_8",),
        "E4": ("G4_8",),
        "E6": ("G4_8",),
        "E8": ("G8_0",),
        "G2_12": ("E12", "T"),
        "G2_4": ("E12", "G2_0"),
        "T": ("G4_0",),
        "U": ("G4_8",),
        "Y0": ("E8",),
        "Y2": ("E10", "U"),
    }
}


def waits(n):
    if n in TIES:
        return TIES[n]
    far = [f"E{k}" for k in range(n // 2, n, 2)]
    near = [f"E{k}" for k in range(2, n // 2, 2)]
    after = {"T": (f"G{n // 4}_0",), "Y2": ("U",), "U": ("T",), far[0]: (f"G{n // 2}_0",), far[1]: (f"G{n // 2}_0",)}
    after.update({b: (a,) for a, b in zip(far, far[2:])})
    after.update({b: (a,) for a, b in zip(far, near)})
    return after


def body(n, x, pair, g, b, w1, b1, w2, b2, w, bias):
    seqs, rows, depth = x.shape
    width = pair.shape[-1]
    hidden = w1.shape[1]
    local, flat, w, mine, theirs = project(
        n, x, pair, g.reshape(1, depth), b.reshape(1, depth),
        w1.T, b1.reshape(1, hidden), w2.T, b2.reshape(1, hidden), w,
    )
    after, done = waits(n), {}
    halves = {h: tuple(o for o in range(0, n, 2) if o & 2 == h) for h in (0, 2)}

    def need(name):
        if name not in done:
            done[name] = make(name)
        return done[name]

    def held(x, name):
        return tie(x, *[need(k) for k in after.get(name, ())])

    def piece(o):
        return need(f"G{o & -o}_{o & (o - 1)}") if o else flat

    def make(name):
        if name == "X":
            return swap(theirs, 1, n)
        if name == "B":
            return pair_up(mine, need("X"))
        if name in ("T", "U"):
            return spread_weights("TU".index(name), held(local, name), w)
        if name[0] == "P":
            return pack([piece(o) for o in halves[int(name[1:])]])
        if name[0] == "Y":
            return swap(held(need("P" + name[1:]), name), 1, n)
        if name[0] == "E":
            k = int(name[1:])
            return swap(held(need("B")[k // 2], name), k, n)
        k, o = map(int, name[1:].split("_"))
        return swap(held(piece(o), name), k, n)

    pieces = [need(f"{a}{h}") for h in halves for a in "PY"]
    places = [tuple(o ^ q for o in halves[h]) for h in halves for q in (0, 1)]
    scale = 1.0 / seqs
    bias = bias.reshape(1, width)
    pair_rows, late = update(places, scale, bias, held(pair, "K"), need("T"), need("U"), pieces)
    chips = tuple(range(0, n, 2))
    return pair_rows, add_turned(chips, [need(f"E{k}") if k else need("B")[0] for k in chips], late)


def solution(mesh):
    pair_spec = P(("grp", "row"), None, None)
    in_specs = (P("grp", "row", None), pair_spec) + (P(),) * 8
    return jax.shard_map(
        functools.partial(body, mesh.shape["row"]),
        mesh=mesh,
        in_specs=in_specs,
        out_specs=(pair_spec, pair_spec),
        check_vma=False,
    )
```
